32 devices in a mesh: seq: 8 (over z, core), chan: 4 (over y, x).
Axes of the slice: x: 2, y: 2, z: 4, core: 2. Of those that a mesh axis runs over, the one named last changes fastest.
Arguments:
- tokens: bfloat16 [2560, 4096], P('seq', 'chan'), may hold values from -70 to 70
- in_weight: bfloat16 [4096, 3, 4096], P(None, None, 'chan'), may hold values from -0.09375 to 0.09375
- short_filter: float32 [3, 3, 4096], P(None, None, 'chan'), may hold values from -2 to 2
- long_filter: bfloat16 [256, 128], P('chan'), may hold values from -0.5 to 0.5
- skip_gain: float32 [4096], P('chan'), may hold values from -4 to 4
- out_weight: bfloat16 [4096, 4096], P('chan'), may hold values from -0.125 to 0.125
Outputs:
- mixed: bfloat16 [2560, 4096], P('seq', 'chan')
The draws below stay inside these ranges and needn't reach their ends.
All inputs are finite; a program needn't handle non-finite values.
Results may differ from the reference program's by a relative error of at most 0.018.
Values may be sent and summed in bfloat16 or wider, within the bound.
A program may use at most 128 MiB of HBM per device.

```python
import math
import jax
import jax.numpy as jnp
from jax import lax

D = 4096
CH = 4096
GROUP = 16
FILT = 128
SHORT = 3
TOKENS = 2560
GROUPS = 256


def draw_tokens(key, part):
    key_list = jax.random.split(key, 3)
    base_values = jnp.clip(jax.random.normal(key_list[0], (TOKENS, D), jnp.float32), -4.0, 4.0)
    row_scale = jnp.exp(jax.random.uniform(key_list[1], (TOKENS, 1), jnp.float32, 0.0, math.log(10.0)))
    column_scale = jnp.exp(jax.random.uniform(key_list[2], (1, D), jnp.float32, 0.0, math.log(10.0)))
    return (base_values * row_scale * column_scale * 0.1).astype(jnp.bfloat16)


def strengthened(drawn, stream_key, source, target, shards_of, factor):
    def block_of(position):
        return (jnp.arange(drawn.shape[position]) // (drawn.shape[position] // shards_of)).reshape((-1,) + (1,) * (drawn.ndim - 1 - position))

    first = jax.random.permutation(stream_key, shards_of)[block_of(target)]
    other_side = (block_of(target) + shards_of // 2) % shards_of
    return jnp.where((block_of(source) == first) | (block_of(source) == other_side), factor * drawn, drawn)


def level_of(key, shape, cuts, smallest, largest):
    def one(dim, blocks):
        steps = jax.random.uniform(jax.random.fold_in(jax.random.fold_in(key, 6), dim), (blocks,), jnp.float32, smallest / len(cuts), largest / len(cuts))
        return jnp.repeat(jnp.exp(steps), shape[dim] // blocks).reshape((-1,) + (1,) * (len(shape) - dim - 1))

    factor_of = one(*cuts[0])
    for cut in cuts[1:]:
        factor_of = factor_of * one(*cut)
    return factor_of


def bell_draw(key, extent, deviation, limit, shards=(), held_as=jnp.bfloat16):
    values = jax.random.normal(key, extent, jnp.float32) * deviation
    if len(shards) > 0:
        values = level_of(key, extent, shards, -0.22, 0.18) * values
    return jnp.clip(values, min=-limit, max=limit).astype(held_as)


def bell_draw_with(rng, shape, width, most, shards, heavy, held_as=jnp.bfloat16):
    result = width * jax.random.normal(rng, shape, jnp.float32)
    if shards:
        result = result * level_of(rng, shape, shards, -0.22, 0.18)
    return jnp.clip(strengthened(result, jax.random.fold_in(rng, 3), *heavy), -most, most).astype(held_as)


def setup_inputs(seed: int = 0) -> dict:
    keys = jax.random.split(jax.random.key(seed), 7)
    tokens = draw_tokens(jax.random.fold_in(keys[6], 71), 0)
    in_weight = bell_draw(keys[1], (D, 3, CH), D ** -0.5, 0.09375, ((2, 4),))
    short_filter = bell_draw(keys[2], (SHORT, 3, CH), 0.4, 2.0, ((2, 4),), jnp.float32)
    long_filter = bell_draw(keys[3], (GROUPS, FILT), 0.09, 0.5, ((0, 4),))
    skip_gain = bell_draw(keys[4], (CH,), 1.0, 4.0, ((0, 4),), jnp.float32)
    out_weight = bell_draw_with(keys[5], (CH, D), CH ** -0.5, 0.125, ((0, 4),), (0, 1, 4, 2.0))
    return dict(tokens=tokens, in_weight=in_weight, short_filter=short_filter, long_filter=long_filter, skip_gain=skip_gain, out_weight=out_weight)


def short_stream(projected, short_filter, stream):
    widened = projected[:, stream, :].astype(jnp.float32)
    padded = jnp.pad(widened, ((SHORT - 1, 0), (0, 0)))
    summed = jnp.zeros((TOKENS, CH), jnp.float32)
    for step_back in range(SHORT):
        summed = summed + short_filter[step_back, stream] * padded[SHORT - 1 - step_back:SHORT - 1 - step_back + TOKENS]
    return summed

def reference(tokens, in_weight, short_filter, long_filter, skip_gain, out_weight):
    panel_sum = jnp.dot(tokens, in_weight.reshape(D, 3 * CH), preferred_element_type=jnp.float32)
    widened = tokens.astype(jnp.float32)
    inverse_rms = lax.rsqrt(lax.optimization_barrier(jnp.mean(widened * widened, axis=1, keepdims=True)) + 1e-06)
    projected = (panel_sum * inverse_rms).astype(jnp.bfloat16).reshape(TOKENS, 3, CH)
    queries = short_stream(projected, short_filter, 0)
    keys_part = short_stream(projected, short_filter, 1)
    values_part = short_stream(projected, short_filter, 2)
    gated = (keys_part * values_part).astype(jnp.bfloat16)
    gated_wide = gated.astype(jnp.float32)
    channel_taps = jnp.repeat(long_filter.astype(jnp.float32), GROUP, axis=0)
    padded = jnp.pad(gated_wide, ((FILT - 1, 0), (0, 0)))

    def add_tap(step_back, summed):
        shifted = lax.dynamic_slice_in_dim(padded, FILT - 1 - step_back, TOKENS, 0)
        return summed + channel_taps[:, step_back] * shifted
    long_mixed = lax.fori_loop(0, FILT, add_tap, jnp.zeros((TOKENS, CH), jnp.float32))
    long_mixed = long_mixed + skip_gain * gated_wide
    hidden = (queries * long_mixed).astype(jnp.bfloat16)
    return jnp.dot(hidden, out_weight, preferred_element_type=jnp.float32).astype(jnp.bfloat16)
```

```python
import functools

import jax
import jax.numpy as jnp
from jax import lax
from jax.experimental import pallas as pl
from jax.experimental.pallas import tpu as pltpu
from jax.sharding import PartitionSpec as P

MESH = pl.DeviceIdType.MESH
F32, BF16 = jnp.float32, jnp.bfloat16
PAD = 8


def kernel(
    n_seq, n_chan, tok, w_hbm, sf, lf, skip, wo_hbm, out,
    panel, wv, wo, acc, ssq, rev, toep, gext, tail, halo_p, hid, psend, precv,
    w_sem, wo_sem, ag_send, ag_recv, rs_send, rs_recv, halo_send, halo_recv,
):
    rows, kc = tok.shape
    cc = w_hbm.shape[2]
    oc = out.shape[1]
    groups, taps = lf.shape
    gsize = cc // groups
    ct = min(256, cc)
    tiles = cc // ct
    gpt = ct // gsize
    ot = min(256, oc)
    model = kc * n_chan
    seq = lax.axis_index("seq")
    chan = lax.axis_index("chan")
    width = 2 if n_chan % 2 == 0 else 1
    height = n_chan // width
    my_y, my_x = chan // width, lax.rem(chan, width)

    def at_offset(d, sign):
        dy, dx = d // width, d % width
        y = lax.rem(my_y + sign * dy + height, height)
        x = lax.rem(my_x + sign * dx + width, width)
        return y * width + x

    target = [at_offset(d, 1) for d in range(n_chan)]
    source = [at_offset(d, -1) for d in range(n_chan)]

    def w_copy(d):
        return pltpu.make_async_copy(
            w_hbm.at[:, pl.ds(pl.multiple_of(source[d] * kc, kc), kc), :], wv.at[d], w_sem.at[d]
        )

    def wo_copy(d):
        return pltpu.make_async_copy(
            wo_hbm.at[:, pl.ds(pl.multiple_of(target[d] * oc, oc), oc)], wo.at[d], wo_sem.at[d]
        )

    def ag_copy(d):
        return pltpu.make_async_remote_copy(
            src_ref=tok, dst_ref=panel.at[d - 1],
            send_sem=ag_send.at[d - 1], recv_sem=ag_recv.at[d - 1],
            device_id=(seq, target[d]), device_id_type=MESH,
        )

    def halo_copy(which):
        src, dst = (
            (tail, halo_p) if which == 0 else (gext.at[pl.ds(rows, taps)], gext.at[pl.ds(0, taps)])
        )
        return pltpu.make_async_remote_copy(
            src_ref=src, dst_ref=dst,
            send_sem=halo_send.at[which], recv_sem=halo_recv.at[which],
            device_id=(lax.rem(seq + 1, n_seq), chan), device_id_type=MESH,
        )

    def rs_copy(part, r0, r1, d):
        return pltpu.make_async_remote_copy(
            src_ref=psend.at[d - 1, pl.ds(r0, r1 - r0)], dst_ref=precv.at[d - 1, pl.ds(r0, r1 - r0)],
            send_sem=rs_send.at[part, d - 1], recv_sem=rs_recv.at[part, d - 1],
            device_id=(seq, target[d]), device_id_type=MESH,
        )

    w_copy(0).start()
    barrier = pltpu.get_barrier_semaphore()
    for d in range(1, n_chan):
        pl.semaphore_signal(barrier, inc=1, device_id=(seq, target[d]), device_id_type=MESH)

    @pl.when(seq > 0)
    def _():
        pl.semaphore_signal(barrier, inc=1, device_id=(seq - 1, chan), device_id_type=MESH)

    @pl.when(seq < n_seq - 1)
    def _():
        pl.semaphore_signal(barrier, inc=1, device_id=(seq + 1, chan), device_id_type=MESH)

    arrivals = n_chan - 1 + (seq > 0).astype(jnp.int32) + (seq < n_seq - 1).astype(jnp.int32)
    pl.semaphore_wait(barrier, arrivals)

    for d in range(n_chan - 1, 0, -1):
        ag_copy(d).start()
    for d in range(1, n_chan):
        w_copy(d).start()
    for d in range(n_chan):
        wo_copy(d).start()

    def add_squares(ref, first):
        total = jnp.zeros((rows, 128), F32)
        for c in range(0, kc, 128):
            part = ref[:, c : c + 128].astype(F32)
            total = total + part * part
        ssq[...] = total if first else ssq[...] + total

    def col(j, size):
        return pl.ds(pl.multiple_of(j * size, size), size)

    add_squares(tok, True)
    w_copy(0).wait()

    @pl.loop(0, tiles)
    def _(j):
        for i in range(3):
            acc[i, PAD : PAD + rows, col(j, ct)] = jnp.dot(
                tok[...], wv[0, i, :, col(j, ct)], preferred_element_type=F32
            )

    lag = lax.broadcasted_iota(jnp.int32, (taps, 2 * taps), 0)
    place = lax.broadcasted_iota(jnp.int32, (taps, 2 * taps), 1)
    flip = jnp.where(lag + place == taps, 1.0, 0.0).astype(BF16)
    rev[...] = jnp.dot(lf[...], flip, preferred_element_type=F32)

    @pl.loop(0, groups)
    def _(g):
        line = jnp.broadcast_to(rev[pl.ds(g, 1), :], (taps, 2 * taps))
        toep[g] = pltpu.roll(line, 0, 1, stride=1, stride_axis=0).astype(BF16)

    gext[pl.ds(taps + rows, gext.shape[0] - taps - rows), :] = jnp.zeros(
        (gext.shape[0] - taps - rows, cc), BF16
    )

    for d in range(1, n_chan):
        ag_copy(d).wait_recv()
        w_copy(d).wait()
        add_squares(panel.at[d - 1], False)
        if d < n_chan - 1:

            @pl.loop(0, tiles)
            def _(j):
                for i in range(3):
                    acc[i, PAD : PAD + rows, col(j, ct)] += jnp.dot(
                        panel[d - 1], wv[d, i, :, col(j, ct)], preferred_element_type=F32
                    )

    last = n_chan - 1
    inverse = lax.rsqrt(jnp.sum(ssq[...], axis=1, keepdims=True) * (1.0 / model) + 1e-6)
    ssq[...] = jnp.broadcast_to(inverse, (rows, 128))

    @pl.loop(0, tiles)
    def _(j):
        scale = ssq[:, 0:1]
        for i in range(3):
            summed = acc[i, PAD : PAD + rows, col(j, ct)] + jnp.dot(
                panel[last - 1], wv[last, i, :, col(j, ct)], preferred_element_type=F32
            )
            projected = (summed * scale).astype(BF16)
            acc[i, PAD : PAD + rows, col(j, ct)] = projected.astype(F32)
            tail[i, :, col(j, ct)] = projected[rows - 16 :]

    @pl.when(seq < n_seq - 1)
    def _():
        halo_copy(0).start()

    def feature(i, r0, r1, c):
        total = sf[0, i : i + 1, c] * acc[i, PAD + r0 : PAD + r1, c]
        for step in range(1, sf.shape[0]):
            total = total + sf[step, i : i + 1, c] * acc[i, PAD + r0 - step : PAD + r1 - step, c]
        return total

    def gate(r0, r1):
        @pl.loop(0, tiles)
        def _(j):
            c = col(j, ct)
            gext[taps + r0 : taps + r1, c] = (feature(1, r0, r1, c) * feature(2, r0, r1, c)).astype(BF16)

    gate(rows - taps, rows)

    @pl.when(seq < n_seq - 1)
    def _():
        halo_copy(1).start()

    gate(16, rows - taps)

    @pl.when(seq > 0)
    def _():
        halo_copy(0).wait_recv()
        for i in range(3):
            acc[i, 0:PAD, :] = halo_p[i, 16 - PAD : 16, :].astype(F32)

    @pl.when(seq == 0)
    def _():
        acc[:, 0:PAD, :] = jnp.zeros((3, PAD, cc), F32)
        gext[0:taps, :] = jnp.zeros((taps, cc), BF16)

    gate(0, 16)

    def long_filter(r0, size):
        @pl.loop(0, tiles)
        def _(j):
            c = col(j, ct)
            table = toep[pl.ds(j * gpt, gpt), 0:size, :].reshape(gpt * size, 2 * taps)
            full = jnp.dot(table, gext[r0 : r0 + 2 * taps, c], preferred_element_type=F32)
            owner = lax.broadcasted_iota(jnp.int32, (size, ct), 1) // gsize
            mixed = full[0:size]
            for k in range(1, gpt):
                mixed = jnp.where(owner == k, full[k * size : (k + 1) * size], mixed)
            gated = gext[taps + r0 : taps + r0 + size, c].astype(F32)
            mixed = mixed + skip[:, c] * gated
            hid[r0 : r0 + size, c] = (feature(0, r0, r0 + size, c) * mixed).astype(BF16)

    def send_part(part, r0, r1):
        for d in range(n_chan - 1, 0, -1):

            @pl.loop(0, oc // ot)
            def _(j):
                psend[d - 1, r0:r1, col(j, ot)] = jnp.dot(
                    hid[r0:r1, :], wo[d, :, col(j, ot)], preferred_element_type=F32
                ).astype(BF16)

            rs_copy(part, r0, r1, d).start()

    for d in range(n_chan):
        wo_copy(d).wait()
    starts = list(range(0, rows, taps))
    for r0 in starts[:0:-1]:
        long_filter(r0, min(taps, rows - r0))
    parts = [(taps, rows), (0, taps)]
    send_part(0, *parts[0])

    @pl.when(seq > 0)
    def _():
        halo_copy(1).wait_recv()

    long_filter(0, taps)
    send_part(1, *parts[1])

    for part, (r0, r1) in enumerate(parts):
        for d in range(n_chan - 1, 0, -1):
            rs_copy(part, r0, r1, d).wait_recv()

        @pl.loop(0, oc // ot)
        def _(j):
            c = col(j, ot)
            total = jnp.dot(hid[r0:r1, :], wo[0, :, c], preferred_element_type=F32)
            for d in range(1, n_chan):
                total = total + precv[d - 1, r0:r1, c].astype(F32)
            out[r0:r1, c] = total.astype(BF16)

    for d in range(1, n_chan):
        ag_copy(d).wait_send()
        for part, (r0, r1) in enumerate(parts):
            rs_copy(part, r0, r1, d).wait_send()

    @pl.when(seq < n_seq - 1)
    def _():
        halo_copy(0).wait_send()
        halo_copy(1).wait_send()


def solution(mesh):
    n_seq, n_chan = mesh.shape["seq"], mesh.shape["chan"]

    def body(tokens, in_weight, short_filter, long_filter, skip_gain, out_weight):
        rows, kc = tokens.shape
        cc = in_weight.shape[2]
        oc = out_weight.shape[1] // n_chan
        groups, taps = long_filter.shape
        streams = jnp.transpose(in_weight, (1, 0, 2))
        ext = taps + -(-rows // taps) * taps
        vmem = pl.BlockSpec(memory_space=pltpu.VMEM)
        hbm = pl.BlockSpec(memory_space=pl.ANY)
        dma = pltpu.SemaphoreType.DMA
        peers = n_chan - 1
        return pl.pallas_call(
            functools.partial(kernel, n_seq, n_chan),
            out_shape=jax.ShapeDtypeStruct((rows, oc), BF16),
            in_specs=[vmem, hbm, vmem, vmem, vmem, hbm],
            out_specs=vmem,
            scratch_shapes=[
                pltpu.VMEM((peers, rows, kc), BF16),
                pltpu.VMEM((n_chan, 3, kc, cc), BF16),
                pltpu.VMEM((n_chan, cc, oc), BF16),
                pltpu.VMEM((3, PAD + rows, cc), F32),
                pltpu.VMEM((rows, 128), F32),
                pltpu.VMEM((groups, 2 * taps), F32),
                pltpu.VMEM((groups, taps, 2 * taps), BF16),
                pltpu.VMEM((ext, cc), BF16),
                pltpu.VMEM((3, 16, cc), BF16),
                pltpu.VMEM((3, 16, cc), BF16),
                pltpu.VMEM((rows, cc), BF16),
                pltpu.VMEM((peers, rows, oc), BF16),
                pltpu.VMEM((peers, rows, oc), BF16),
                dma((n_chan,)),
                dma((n_chan,)),
                dma((peers,)),
                dma((peers,)),
                dma((2, peers)),
                dma((2, peers)),
                dma((2,)),
                dma((2,)),
            ],
            compiler_params=pltpu.CompilerParams(
                collective_id=0, has_side_effects=True, vmem_limit_bytes=62 * 2**20
            ),
            cost_estimate=pl.CostEstimate(
                flops=2 * rows * cc * (kc * n_chan * 3 + oc * n_chan),
                bytes_accessed=2 * (in_weight.size + out_weight.size),
                transcendentals=0,
            ),
        )(tokens, streams, short_filter, long_filter, skip_gain.reshape(1, cc), out_weight)

    in_specs = (
        P("seq", "chan"),
        P(None, None, "chan"),
        P(None, None, "chan"),
        P("chan", None),
        P("chan"),
        P("chan", None),
    )
    return jax.shard_map(body, mesh=mesh, in_specs=in_specs, out_specs=P("seq", "chan"), check_vma=False)
```

```python
import functools

import jax
import jax.numpy as jnp
from jax import lax
from jax.experimental import pallas as pl
from jax.experimental.pallas import tpu as pltpu
from jax.sharding import PartitionSpec as P

MESH = pl.DeviceIdType.MESH
F32, BF16 = jnp.float32, jnp.bfloat16
PAD = 8


def kernel(
    n_seq, n_chan, tok, w_hbm, sf, lf, skip, wo_hbm, out,
    panel, wv, wo, acc, ssq, rev, toep, gext, tail, halo_p, hid, psend, precv, relay,
    w_sem, wo_sem, ag_send, ag_recv, rs_send, rs_recv, halo_send, halo_recv,
):
    rows, kc = tok.shape
    cc = w_hbm.shape[2]
    oc = out.shape[1]
    groups, taps = lf.shape
    gsize = cc // groups
    ct = min(256, cc)
    tiles = cc // ct
    gpt = ct // gsize
    ot = min(256, oc)
    model = kc * n_chan
    seq = lax.axis_index("seq")
    chan = lax.axis_index("chan")
    width = 2 if n_chan % 2 == 0 else 1
    height = n_chan // width
    my_y, my_x = chan // width, lax.rem(chan, width)

    def at_offset(d, sign):
        dy, dx = d // width, d % width
        y = lax.rem(my_y + sign * dy + height, height)
        x = lax.rem(my_x + sign * dx + width, width)
        return y * width + x

    target = [at_offset(d, 1) for d in range(n_chan)]
    source = [at_offset(d, -1) for d in range(n_chan)]

    def w_copy(d):
        return pltpu.make_async_copy(
            w_hbm.at[:, pl.ds(pl.multiple_of(source[d] * kc, kc), kc), :], wv.at[d], w_sem.at[d]
        )

    def wo_copy(d):
        return pltpu.make_async_copy(
            wo_hbm.at[:, pl.ds(pl.multiple_of(target[d] * oc, oc), oc)], wo.at[d], wo_sem.at[d]
        )

    square = width == 2 and height == 2
    top, bottom = pl.ds(0, rows // 2), pl.ds(rows // 2, rows // 2)
    left, right = pl.ds(0, oc // 2), pl.ds(oc // 2, oc // 2)

    def push(src, dst, send, recv, d):
        return pltpu.make_async_remote_copy(
            src_ref=src, dst_ref=dst, send_sem=send, recv_sem=recv,
            device_id=(seq, target[d]), device_id_type=MESH,
        )

    def ag_copy(k):
        if square:
            src, dst, d = (
                (tok.at[top], panel.at[0, top], 1),
                (tok.at[bottom], panel.at[1, bottom], 2),
                (tok.at[bottom], panel.at[0, bottom], 1),
                (tok.at[top], panel.at[1, top], 2),
                (panel.at[0, top], panel.at[2, top], 2),
                (panel.at[1, bottom], panel.at[2, bottom], 1),
            )[k]
        else:
            src, dst, d = tok, panel.at[k], k + 1
        return push(src, dst, ag_send.at[k], ag_recv.at[k], d)

    def rs_copy(part, k):
        r0, r1 = parts[part]
        r = pl.ds(r0, r1 - r0)
        if square:
            src, dst, d = (
                (psend.at[2, r, left], relay.at[0, r], 1),
                (psend.at[2, r, right], relay.at[1, r], 2),
                (psend.at[0, r, left], precv.at[0, r, left], 1),
                (psend.at[1, r, right], precv.at[1, r, right], 2),
                (psend.at[1, r, left], precv.at[1, r, left], 2),
                (psend.at[0, r, right], precv.at[0, r, right], 1),
            )[k]
        else:
            src, dst, d = psend.at[k, r], precv.at[k, r], k + 1
        return push(src, dst, rs_send.at[part, k], rs_recv.at[part, k], d)

    ag_count = rs_count = 6 if square else n_chan - 1
    arriving = 2 if square else n_chan - 1
    starts = list(range(0, rows, taps))
    parts = [(r0, min(rows, r0 + taps)) for r0 in starts[::-1]]

    def halo_copy(which):
        src, dst = (
            (tail, halo_p) if which == 0 else (gext.at[pl.ds(rows, taps)], gext.at[pl.ds(0, taps)])
        )
        return pltpu.make_async_remote_copy(
            src_ref=src, dst_ref=dst,
            send_sem=halo_send.at[which], recv_sem=halo_recv.at[which],
            device_id=(lax.rem(seq + 1, n_seq), chan), device_id_type=MESH,
        )

    w_copy(0).start()
    barrier = pltpu.get_barrier_semaphore()
    for d in range(1, n_chan):
        pl.semaphore_signal(barrier, inc=1, device_id=(seq, target[d]), device_id_type=MESH)

    @pl.when(seq > 0)
    def _():
        pl.semaphore_signal(barrier, inc=1, device_id=(seq - 1, chan), device_id_type=MESH)

    @pl.when(seq < n_seq - 1)
    def _():
        pl.semaphore_signal(barrier, inc=1, device_id=(seq + 1, chan), device_id_type=MESH)

    arrivals = n_chan - 1 + (seq > 0).astype(jnp.int32) + (seq < n_seq - 1).astype(jnp.int32)
    pl.semaphore_wait(barrier, arrivals)

    for k in range(4 if square else ag_count):
        ag_copy(k).start()
    for d in range(1, n_chan):
        w_copy(d).start()
    for d in range(n_chan):
        wo_copy(d).start()

    def add_squares(ref, first):
        total = jnp.zeros((rows, 128), F32)
        for c in range(0, kc, 128):
            part = ref[:, c : c + 128].astype(F32)
            total = total + part * part
        ssq[...] = total if first else ssq[...] + total

    def col(j, size):
        return pl.ds(pl.multiple_of(j * size, size), size)

    add_squares(tok, True)
    w_copy(0).wait()

    @pl.loop(0, tiles)
    def _(j):
        for i in range(3):
            acc[i, PAD : PAD + rows, col(j, ct)] = jnp.dot(
                tok[...], wv[0, i, :, col(j, ct)], preferred_element_type=F32
            )

    if square:
        ag_copy(0).wait_recv()
        ag_copy(4).start()
        ag_copy(1).wait_recv()
        ag_copy(5).start()

    lag = lax.broadcasted_iota(jnp.int32, (taps, 2 * taps), 0)
    place = lax.broadcasted_iota(jnp.int32, (taps, 2 * taps), 1)
    flip = jnp.where(lag + place == taps, 1.0, 0.0).astype(BF16)
    rev[...] = jnp.dot(lf[...], flip, preferred_element_type=F32)

    @pl.loop(0, groups)
    def _(g):
        line = jnp.broadcast_to(rev[pl.ds(g, 1), :], (taps, 2 * taps))
        toep[g] = pltpu.roll(line, 0, 1, stride=1, stride_axis=0).astype(BF16)

    gext[pl.ds(taps + rows, gext.shape[0] - taps - rows), :] = jnp.zeros(
        (gext.shape[0] - taps - rows, cc), BF16
    )

    for d in range(1, n_chan):
        for k in ((2,), (3,), (4, 5))[d - 1] if square else (d - 1,):
            ag_copy(k).wait_recv()
        w_copy(d).wait()
        add_squares(panel.at[d - 1], False)
        if d < n_chan - 1:

            @pl.loop(0, tiles)
            def _(j):
                for i in range(3):
                    acc[i, PAD : PAD + rows, col(j, ct)] += jnp.dot(
                        panel[d - 1], wv[d, i, :, col(j, ct)], preferred_element_type=F32
                    )

    last = n_chan - 1
    inverse = lax.rsqrt(jnp.sum(ssq[...], axis=1, keepdims=True) * (1.0 / model) + 1e-6)
    ssq[...] = jnp.broadcast_to(inverse, (rows, 128))

    @pl.loop(0, tiles)
    def _(j):
        scale = ssq[:, 0:1]
        for i in range(3):
            summed = acc[i, PAD : PAD + rows, col(j, ct)] + jnp.dot(
                panel[last - 1], wv[last, i, :, col(j, ct)], preferred_element_type=F32
            )
            projected = (summed * scale).astype(BF16)
            acc[i, PAD : PAD + rows, col(j, ct)] = projected.astype(F32)
            tail[i, :, col(j, ct)] = projected[rows - 16 :]

    @pl.when(seq < n_seq - 1)
    def _():
        halo_copy(0).start()

    def feature(i, r0, r1, c):
        total = sf[0, i : i + 1, c] * acc[i, PAD + r0 : PAD + r1, c]
        for step in range(1, sf.shape[0]):
            total = total + sf[step, i : i + 1, c] * acc[i, PAD + r0 - step : PAD + r1 - step, c]
        return total

    def gate(r0, r1):
        @pl.loop(0, tiles)
        def _(j):
            c = col(j, ct)
            gext[taps + r0 : taps + r1, c] = (feature(1, r0, r1, c) * feature(2, r0, r1, c)).astype(BF16)

    gate(rows - taps, rows)

    @pl.when(seq < n_seq - 1)
    def _():
        halo_copy(1).start()

    gate(16, rows - taps)

    @pl.when(seq > 0)
    def _():
        halo_copy(0).wait_recv()
        for i in range(3):
            acc[i, 0:PAD, :] = halo_p[i, 16 - PAD : 16, :].astype(F32)

    @pl.when(seq == 0)
    def _():
        acc[:, 0:PAD, :] = jnp.zeros((3, PAD, cc), F32)
        gext[0:taps, :] = jnp.zeros((taps, cc), BF16)

    gate(0, 16)

    def long_filter(r0, size):
        @pl.loop(0, tiles)
        def _(j):
            c = col(j, ct)
            table = toep[pl.ds(j * gpt, gpt), 0:size, :].reshape(gpt * size, 2 * taps)
            full = jnp.dot(table, gext[r0 : r0 + 2 * taps, c], preferred_element_type=F32)
            owner = lax.broadcasted_iota(jnp.int32, (size, ct), 1) // gsize
            mixed = full[0:size]
            for k in range(1, gpt):
                mixed = jnp.where(owner == k, full[k * size : (k + 1) * size], mixed)
            gated = gext[taps + r0 : taps + r0 + size, c].astype(F32)
            mixed = mixed + skip[:, c] * gated
            hid[r0 : r0 + size, c] = (feature(0, r0, r0 + size, c) * mixed).astype(BF16)

    def send_part(part):
        r0, r1 = parts[part]

        def partial(d, first, count):
            @pl.loop(first // ot, (first + count) // ot)
            def _(j):
                psend[d - 1, r0:r1, col(j, ot)] = jnp.dot(
                    hid[r0:r1, :], wo[d, :, col(j, ot)], preferred_element_type=F32
                ).astype(BF16)

        if square:
            partial(3, 0, oc)
            rs_copy(part, 0).start()
            rs_copy(part, 1).start()
            partial(1, 0, oc)
            rs_copy(part, 2).start()
            partial(2, 0, oc)
            rs_copy(part, 3).start()
        else:
            for d in range(n_chan - 1, 0, -1):
                partial(d, 0, oc)
                rs_copy(part, d - 1).start()

    def relay_part(part):
        r0, r1 = parts[part]
        for k, slot, c in ((0, 1, left), (1, 0, right)):
            rs_copy(part, k).wait_recv()
            psend[slot, r0:r1, c] = (
                psend[slot, r0:r1, c].astype(F32) + relay[k, r0:r1].astype(F32)
            ).astype(BF16)
            rs_copy(part, 4 + k).start()

    for d in range(n_chan):
        wo_copy(d).wait()
    for part, (r0, r1) in enumerate(parts):
        if r0 == 0:

            @pl.when(seq > 0)
            def _():
                halo_copy(1).wait_recv()

        long_filter(r0, r1 - r0)
        send_part(part)
        if square and part > 0:
            relay_part(part - 1)
    if square:
        relay_part(len(parts) - 1)

    for part, (r0, r1) in enumerate(parts):
        for k in range(2, 6) if square else range(rs_count):
            rs_copy(part, k).wait_recv()

        @pl.loop(0, oc // ot)
        def _(j):
            c = col(j, ot)
            total = jnp.dot(hid[r0:r1, :], wo[0, :, c], preferred_element_type=F32)
            for k in range(arriving):
                total = total + precv[k, r0:r1, c].astype(F32)
            out[r0:r1, c] = total.astype(BF16)

    for k in range(ag_count):
        ag_copy(k).wait_send()
    for part in range(len(parts)):
        for k in range(rs_count):
            rs_copy(part, k).wait_send()

    @pl.when(seq < n_seq - 1)
    def _():
        halo_copy(0).wait_send()
        halo_copy(1).wait_send()


def solution(mesh):
    n_seq, n_chan = mesh.shape["seq"], mesh.shape["chan"]

    def body(tokens, in_weight, short_filter, long_filter, skip_gain, out_weight):
        rows, kc = tokens.shape
        cc = in_weight.shape[2]
        oc = out_weight.shape[1] // n_chan
        groups, taps = long_filter.shape
        streams = jnp.transpose(in_weight, (1, 0, 2))
        ext = taps + -(-rows // taps) * taps
        vmem = pl.BlockSpec(memory_space=pltpu.VMEM)
        hbm = pl.BlockSpec(memory_space=pl.ANY)
        dma = pltpu.SemaphoreType.DMA
        peers = n_chan - 1
        return pl.pallas_call(
            functools.partial(kernel, n_seq, n_chan),
            out_shape=jax.ShapeDtypeStruct((rows, oc), BF16),
            in_specs=[vmem, hbm, vmem, vmem, vmem, hbm],
            out_specs=vmem,
            scratch_shapes=[
                pltpu.VMEM((peers, rows, kc), BF16),
                pltpu.VMEM((n_chan, 3, kc, cc), BF16),
                pltpu.VMEM((n_chan, cc, oc), BF16),
                pltpu.VMEM((3, PAD + rows, cc), F32),
                pltpu.VMEM((rows, 128), F32),
                pltpu.VMEM((groups, 2 * taps), F32),
                pltpu.VMEM((groups, taps, 2 * taps), BF16),
                pltpu.VMEM((ext, cc), BF16),
                pltpu.VMEM((3, 16, cc), BF16),
                pltpu.VMEM((3, 16, cc), BF16),
                pltpu.VMEM((rows, cc), BF16),
                pltpu.VMEM((peers, rows, oc), BF16),
                pltpu.VMEM((peers, rows, oc), BF16),
                pltpu.VMEM((2, rows, oc // 2), BF16),
                dma((n_chan,)),
                dma((n_chan,)),
                dma((max(6, peers),)),
                dma((max(6, peers),)),
                dma((-(-rows // taps), max(6, peers))),
                dma((-(-rows // taps), max(6, peers))),
                dma((2,)),
                dma((2,)),
            ],
            compiler_params=pltpu.CompilerParams(
                collective_id=0, has_side_effects=True, vmem_limit_bytes=62 * 2**20
            ),
            cost_estimate=pl.CostEstimate(
                flops=2 * rows * cc * (kc * n_chan * 3 + oc * n_chan),
                bytes_accessed=2 * (in_weight.size + out_weight.size),
                transcendentals=0,
            ),
        )(tokens, streams, short_filter, long_filter, skip_gain.reshape(1, cc), out_weight)

    in_specs = (
        P("seq", "chan"),
        P(None, None, "chan"),
        P(None, None, "chan"),
        P("chan", None),
        P("chan"),
        P("chan", None),
    )
    return jax.shard_map(body, mesh=mesh, in_specs=in_specs, out_specs=P("seq", "chan"), check_vma=False)
```
